512 devices in a mesh: grp: 32 (over y_lo, z, core), seq: 16 (over x, y_hi).
Axes of the slice: x: 4, y: 8 (y_hi: 4, y_lo: 2; y = y_hi * 2 + y_lo), z: 8, core: 2. Of those that a mesh axis runs over, the one named last changes fastest.
Arguments:
- query: bfloat16 [131072, 1280], P(('grp', 'seq')), may hold values from -64 to 64
- keys: bfloat16 [131072, 1280], P(('grp', 'seq')), may hold values from -4 to 4
- values: bfloat16 [131072, 1280], P(('grp', 'seq')), may hold values from -5 to 5
- cotangent: bfloat16 [131072, 1280], P(('grp', 'seq')), may hold values from -5 to 5
Outputs:
- attended: bfloat16 [131072, 1280], P(('grp', 'seq'))
- query_grad: bfloat16 [131072, 1280], P(('grp', 'seq'))
- key_grad: bfloat16 [131072, 1280], P(('grp', 'seq'))
- value_grad: bfloat16 [131072, 1280], P(('grp', 'seq'))
The draws below stay inside these ranges and needn't reach their ends.
All inputs are finite; a program needn't handle non-finite values.
Results may differ from the reference program's by a relative error of at most 0.022.
Values may be sent and summed in bfloat16 or wider, within the bound.
A program may use at most 128 MiB of HBM per device.

```python
import math
import jax
import jax.numpy as jnp
from jax import lax

HEADS = 16
D = 1280
FINE = 256
POOL = 16
COARSE = 16
TOKENS = 131072
N_SEQ = 16


def shared_keys(key):
    first = jax.random.fold_in(key, 0)
    normal_part = jnp.clip(jax.random.normal(first, (TOKENS, D), jnp.float32), -4.0, 4.0)
    return normal_part


def draw_keys(key, part):
    return shared_keys(key).astype(jnp.bfloat16)


def draw_query(key, part):
    own_key = jax.random.fold_in(key, 5)
    noise = jnp.clip(jax.random.normal(own_key, (TOKENS, D), jnp.float32), -4.0, 4.0)
    return (1.5 * noise).astype(jnp.bfloat16)


def shard_levels(rng, extent, cuts, low, high):
    level, own = 1.0, jax.random.fold_in(rng, 6)
    for dim, parts in cuts:
        steps = jnp.exp(jax.random.uniform(jax.random.fold_in(own, dim), (parts,), jnp.float32, low / len(cuts), high / len(cuts)))
        level = level * jnp.repeat(steps, extent[dim] // parts).reshape([-1 if axis == dim else 1 for axis in range(len(extent))])
    return level


def bell_draw(key, shape, spread, reach, cuts=(), kind=jnp.bfloat16):
    array = spread * jax.random.normal(key, shape, jnp.float32)
    if cuts:
        array = array * shard_levels(key, shape, cuts, -0.22, 0.18)
    return jnp.clip(array, -reach, reach).astype(kind)


def setup_inputs(seed: int = 0) -> dict:
    streams_of = jax.random.split(jax.random.key(seed), 5)
    query = draw_query(jax.random.fold_in(streams_of[4], 71), 0)
    keys = draw_keys(jax.random.fold_in(streams_of[4], 71), 0)
    values = bell_draw(streams_of[2], (TOKENS, D), 1.0, 5.0, ((0, 512),))
    cotangent = bell_draw(streams_of[3], (TOKENS, D), 1.0, 5.0, ((0, 512),))
    return {"query": query, "keys": keys, "values": values, "cotangent": cotangent}


SCORE_FLOOR = -1e+30

def split_heads(matrix, heads):
    return matrix.reshape(matrix.shape[0], heads, matrix.shape[1] // heads)

def head_slice(matrix, index, group_heads):
    return lax.dynamic_slice_in_dim(matrix, index * group_heads, group_heads, 1)

def pooled(matrix, width):
    summed = matrix.astype(jnp.float32).reshape(-1, width, matrix.shape[1]).sum(axis=1)
    return (summed / math.sqrt(width)).astype(jnp.bfloat16)

def visibility(block, rows, n_seq, coarse, devices):
    group = block // n_seq
    member = block % n_seq
    row_ids = jnp.arange(rows, dtype=jnp.int32)[:, None]
    col_ids = jnp.arange(rows, dtype=jnp.int32)[None, :]
    before = jnp.broadcast_to(block > 0, (rows, rows))
    inside = col_ids <= row_ids
    owner = jnp.arange(n_seq * coarse, dtype=jnp.int32) // coarse
    middle = jnp.broadcast_to((owner < member)[None, :], (rows, n_seq * coarse))
    far_ids = jnp.arange(devices, dtype=jnp.int32)
    distant = jnp.broadcast_to((far_ids < jnp.minimum(group * n_seq, block - 1))[None, :], (rows, devices))
    return jnp.concatenate([before, inside, middle, distant], axis=1)

def forward_block(query, keys_all, values_all, visible, heads):
    group_heads = 2
    rows = query.shape[0]
    scale = 1.0 / math.sqrt(query.shape[1] // heads)
    query_h = split_heads(query, heads)
    keys_h = split_heads(keys_all, heads)
    values_h = split_heads(values_all, heads)

    def one_group(index):
        query_g = head_slice(query_h, index, group_heads).astype(jnp.float32)
        keys_g = head_slice(keys_h, index, group_heads).astype(jnp.float32)
        values_g = head_slice(values_h, index, group_heads).astype(jnp.float32)
        scores = jnp.einsum('qhe,khe->hqk', query_g, keys_g) * scale
        scores = jnp.where(visible[None], scores, SCORE_FLOOR)
        top = lax.optimization_barrier(jnp.max(scores, axis=2, keepdims=True))
        expo = jnp.exp(scores - top)
        total = lax.optimization_barrier(jnp.sum(expo, axis=2, keepdims=True))
        weights = (expo / total).astype(jnp.bfloat16)
        mixed = jnp.einsum('hqk,khe->qhe', weights.astype(jnp.float32), values_g)
        return (mixed, (top + jnp.log(total))[:, :, 0])
    mixed, lse = lax.map(one_group, jnp.arange(heads // group_heads, dtype=jnp.int32))
    attended = jnp.moveaxis(mixed, 0, 1).reshape(rows, -1).astype(jnp.bfloat16)
    return (attended, lse.reshape(heads, rows))

def head_products(cotangent, attended, heads):
    rows = cotangent.shape[0]
    product = cotangent.astype(jnp.float32) * attended.astype(jnp.float32)
    return product.reshape(rows, heads, -1).sum(axis=2).T

def backward_block(query, keys_all, values_all, visible, cotangent, lse, delta, heads, skip):
    group_heads = 2
    rows = query.shape[0]
    scale = 1.0 / math.sqrt(query.shape[1] // heads)
    query_h = split_heads(query, heads)
    keys_h = split_heads(keys_all, heads)
    values_h = split_heads(values_all, heads)
    cot_h = split_heads(cotangent, heads)

    def one_group(index):
        query_g = head_slice(query_h, index, group_heads).astype(jnp.float32)
        keys_g = head_slice(keys_h, index, group_heads).astype(jnp.float32)
        values_g = head_slice(values_h, index, group_heads).astype(jnp.float32)
        cot_g = head_slice(cot_h, index, group_heads).astype(jnp.float32)
        lse_g = lax.dynamic_slice_in_dim(lse, index * group_heads, group_heads, 0)
        delta_g = lax.dynamic_slice_in_dim(delta, index * group_heads, group_heads, 0)
        scores = jnp.einsum('qhe,khe->hqk', query_g, keys_g) * scale
        scores = jnp.where(visible[None], scores, SCORE_FLOOR)
        probs = jnp.exp(scores - lse_g[:, :, None])
        dprob = jnp.einsum('qhe,khe->hqk', cot_g, values_g)
        dscore = (probs * (dprob - delta_g[:, :, None])).astype(jnp.bfloat16).astype(jnp.float32)
        weights = probs.astype(jnp.bfloat16).astype(jnp.float32)
        query_part = jnp.einsum('hqk,khe->qhe', dscore, keys_g) * scale
        key_part = jnp.einsum('hqk,qhe->khe', dscore[:, :, skip:], query_g) * scale
        value_part = jnp.einsum('hqk,qhe->khe', weights[:, :, skip:], cot_g)
        return (query_part, key_part, value_part)
    query_part, key_part, value_part = lax.map(one_group, jnp.arange(heads // group_heads, dtype=jnp.int32))
    query_grad = jnp.moveaxis(query_part, 0, 1).reshape(rows, -1)
    key_grad = jnp.moveaxis(key_part, 0, 1).reshape(key_part.shape[1], -1)
    value_grad = jnp.moveaxis(value_part, 0, 1).reshape(value_part.shape[1], -1)
    return (query_grad, key_grad, value_grad)

def rounded(matrix):
    return lax.optimization_barrier(matrix.astype(jnp.bfloat16)).astype(jnp.float32)

def reference(query, keys, values, cotangent):
    blocks = TOKENS // FINE
    group_rows = N_SEQ * COARSE
    mid_keys = pooled(keys, POOL)
    mid_values = pooled(values, POOL)
    far_keys = pooled(mid_keys, COARSE)
    far_values = pooled(mid_values, COARSE)
    block_ids = jnp.arange(blocks, dtype=jnp.int32)

    def assemble(block):
        group = block // N_SEQ
        start = (block * FINE).astype(jnp.int32)
        earlier = (jnp.maximum(block - 1, 0) * FINE).astype(jnp.int32)
        table = (group * group_rows).astype(jnp.int32)
        keys_all = jnp.concatenate([lax.dynamic_slice_in_dim(keys, earlier, FINE, 0), lax.dynamic_slice_in_dim(keys, start, FINE, 0), lax.dynamic_slice_in_dim(mid_keys, table, group_rows, 0), far_keys], axis=0)
        values_all = jnp.concatenate([lax.dynamic_slice_in_dim(values, earlier, FINE, 0), lax.dynamic_slice_in_dim(values, start, FINE, 0), lax.dynamic_slice_in_dim(mid_values, table, group_rows, 0), far_values], axis=0)
        return (start, keys_all, values_all)

    def forward_one(block):
        start, keys_all, values_all = assemble(block)
        query_b = lax.dynamic_slice_in_dim(query, start, FINE, 0)
        return forward_block(query_b, keys_all, values_all, visibility(block, FINE, N_SEQ, COARSE, blocks), HEADS)
    attended, lse = lax.map(forward_one, block_ids)
    attended = attended.reshape(TOKENS, D)

    def backward_one(carry, block):
        next_k, next_v, acc_mid_k, acc_mid_v, acc_far_k, acc_far_v = carry
        start, keys_all, values_all = assemble(block)
        query_b = lax.dynamic_slice_in_dim(query, start, FINE, 0)
        cot_b = lax.dynamic_slice_in_dim(cotangent, start, FINE, 0)
        out_b = lax.dynamic_slice_in_dim(attended, start, FINE, 0)
        lse_b = lax.dynamic_index_in_dim(lse, block, 0, keepdims=False)
        delta_b = head_products(cot_b, out_b, HEADS)
        visible = visibility(block, FINE, N_SEQ, COARSE, blocks)
        query_grad, key_grad, value_grad = backward_block(query_b, keys_all, values_all, visible, cot_b, lse_b, delta_b, HEADS, 0)
        own_k = key_grad[FINE:2 * FINE] + next_k
        own_v = value_grad[FINE:2 * FINE] + next_v
        table = (block // N_SEQ * group_rows).astype(jnp.int32)
        mid_k = lax.dynamic_slice_in_dim(acc_mid_k, table, group_rows, 0) + rounded(key_grad[2 * FINE:2 * FINE + group_rows])
        mid_v = lax.dynamic_slice_in_dim(acc_mid_v, table, group_rows, 0) + rounded(value_grad[2 * FINE:2 * FINE + group_rows])
        acc_mid_k = lax.dynamic_update_slice_in_dim(acc_mid_k, mid_k, table, 0)
        acc_mid_v = lax.dynamic_update_slice_in_dim(acc_mid_v, mid_v, table, 0)
        acc_far_k = acc_far_k + rounded(key_grad[2 * FINE + group_rows:])
        acc_far_v = acc_far_v + rounded(value_grad[2 * FINE + group_rows:])
        carry = (key_grad[:FINE], value_grad[:FINE], acc_mid_k, acc_mid_v, acc_far_k, acc_far_v)
        return (carry, (query_grad.astype(jnp.bfloat16), own_k, own_v))
    start_carry = (jnp.zeros((FINE, D), jnp.float32), jnp.zeros((FINE, D), jnp.float32), jnp.zeros((TOKENS // POOL, D), jnp.float32), jnp.zeros((TOKENS // POOL, D), jnp.float32), jnp.zeros((blocks, D), jnp.float32), jnp.zeros((blocks, D), jnp.float32))
    carry, outputs = lax.scan(backward_one, start_carry, block_ids, reverse=True)
    acc_mid_k, acc_mid_v, acc_far_k, acc_far_v = (carry[2], carry[3], carry[4], carry[5])
    query_grad, fine_k, fine_v = outputs
    spread_k = (acc_mid_k + jnp.repeat(acc_far_k, COARSE, axis=0) / math.sqrt(COARSE)) / math.sqrt(POOL)
    spread_v = (acc_mid_v + jnp.repeat(acc_far_v, COARSE, axis=0) / math.sqrt(COARSE)) / math.sqrt(POOL)
    key_grad = (fine_k.reshape(TOKENS, D) + jnp.repeat(spread_k, POOL, axis=0)).astype(jnp.bfloat16)
    value_grad = (fine_v.reshape(TOKENS, D) + jnp.repeat(spread_v, POOL, axis=0)).astype(jnp.bfloat16)
    return (attended, query_grad.reshape(TOKENS, D), key_grad, value_grad)
```

```python
import functools
import math

import jax
import jax.numpy as jnp
from jax import lax
from jax.experimental import pallas as pl
from jax.experimental.pallas import tpu as pltpu
from jax.sharding import PartitionSpec as P

HEADS = 16
POOL = 16
HALVES = 2
TILE = 128
WINDOW = 256
PAIR = 2
FLOOR = -1e30
LOG2E = 1.4426950408889634
MESH = pl.DeviceIdType.MESH
F32 = jnp.float32
BF16 = jnp.bfloat16


def dot(a, b):
    return jnp.dot(a, b, preferred_element_type=F32)


def kernel(
    n_grp, n_seq,
    q_hbm, k_hbm, v_hbm, c_hbm,
    o_hbm, dq_hbm, dk_hbm, dv_hbm,
    kv, qc, qn, kvt, qc_t, bias, score, weight, dscore,
    out_t, dq_t, out_rows, stat, stat_next, own, mid_part, far_part,
    core_in, core_sum, far_in, far_rows, far_rows_in,
    mid_x_in, mid_x, mid_y_in, grad_rows, far_mine, far_all, padded,
    load_sem, row_send, row_recv, y_send, y_recv, key_send, key_recv, query_send, query_recv, x_send, x_recv, z_send, z_recv,
    pair_send, pair_recv, stat_send, stat_recv, core_send, core_recv,
    mx_send, mx_recv, my_send, my_recv, fz_send, fz_recv, fs_send, fs_recv, store_sem,
):
    rows = q_hbm.shape[0]
    width = q_hbm.shape[1]
    part = width // HALVES
    heads = HEADS // HALVES
    depth = width // HEADS
    coarse = rows // POOL
    mid_rows = n_seq * coarse
    n_far = n_grp * n_seq
    half = n_far // 2
    y_n = math.isqrt(n_seq)
    x_n = n_seq // y_n
    z_n = n_grp // 2
    mid_at = 2 * rows
    far_at = mid_at + mid_rows
    scale = 1.0 / math.sqrt(depth)
    to_log2 = scale * LOG2E
    tiles = part // TILE

    g = lax.axis_index("grp")
    m = lax.axis_index("seq")
    core = g % 2
    zz = g // 2
    xx = m // y_n
    yy = m % y_n
    block = g * n_seq + m
    n_blocks = n_grp * n_seq
    after = (block + 1) % n_blocks
    before = (block + n_blocks - 1) % n_blocks
    next_id = (after // n_seq, after % n_seq)
    prev_id = (before // n_seq, before % n_seq)
    twin_id = (2 * zz + 1 - core, m)

    def y_peer(d):
        return (yy + d) % y_n

    def x_peer(d):
        return (xx + d) % x_n

    def z_peer(i):
        return (zz + i) % z_n

    def remote(src, dst, send, recv, device):
        return pltpu.make_async_remote_copy(
            src_ref=src, dst_ref=dst, send_sem=send, recv_sem=recv,
            device_id=device, device_id_type=MESH,
        )

    def aligned(start, unit):
        return pl.multiple_of(start, unit)

    loads = []
    for c in range(HALVES):
        cols = pl.ds(c * part, part)
        for kind, (ref, dst) in enumerate((
            (k_hbm, kv.at[c, 0, pl.ds(rows, rows)]), (v_hbm, kv.at[c, 1, pl.ds(rows, rows)]),
            (q_hbm, qc.at[c, 0]), (c_hbm, qc.at[c, 1]),
        )):
            loads.append(pltpu.make_async_copy(ref.at[:, cols], dst, load_sem.at[c * 4 + kind]))
    for copy in loads:
        copy.start()

    barrier = pltpu.get_barrier_semaphore()

    def greet(device):
        pl.semaphore_signal(barrier, inc=1, device_id=device, device_id_type=MESH)

    def greet_seq(i, carry):
        greet((g, (m + i) % n_seq))
        return carry

    def greet_z(i, carry):
        greet((2 * z_peer(i) + core, m))
        return carry

    lax.fori_loop(1, n_seq, greet_seq, 0)
    lax.fori_loop(1, z_n, greet_z, 0)
    greet(twin_id)
    greet(next_id)
    greet(prev_id)

    for c in range(HALVES):
        for kind in range(2):
            loads[c * 4 + kind].wait()

    def pooling(n, count):
        row = lax.broadcasted_iota(jnp.int32, (n, n * count), 0)
        col = lax.broadcasted_iota(jnp.int32, (n, n * count), 1)
        return jnp.where((col >= row * count) & (col < row * count + count), 1.0, 0.0).astype(BF16)

    own_mid = pl.ds(aligned(mid_at + m * coarse, coarse), coarse)
    pool_mid = pooling(coarse, POOL)
    for c in range(HALVES):
        for kind in range(2):
            summed = dot(pool_mid, kv[c, kind, rows : 2 * rows, :])
            pooled = (summed / math.sqrt(POOL)).astype(BF16)
            kv[c, kind, own_mid, :] = pooled
            row = jnp.sum(pooled.astype(F32), axis=0, keepdims=True) / math.sqrt(coarse)
            row = row.astype(BF16).astype(F32)
            for t in range(tiles):
                at = c * 16 + kind * 8 + t
                far_mine[at : at + 1, :] = row[:, t * TILE : (t + 1) * TILE]

    pl.semaphore_wait(barrier, (n_seq - 1) + (z_n - 1) + 3)

    def row_copy(i, source, device):
        spot = far_all.at[pl.ds(aligned(source * 32, 32), 32), :]
        return remote(far_mine, spot, row_send.at[i], row_recv.at[i], device)

    def send_row(i, carry):
        row_copy(i, m, (g, (m + i) % n_seq)).start()
        return carry

    lax.fori_loop(1, n_seq, send_row, 0)
    far_all[pl.ds(aligned(m * 32, 32), 32), :] = far_mine[...]

    def mid_slot(member_start, count):
        return pl.ds(aligned(mid_at + member_start * coarse, coarse), count * coarse)

    y_copies = []
    for d in range(1, y_n):
        spot = kv.at[:, :, own_mid, :]
        copy = remote(spot, spot, y_send.at[d], y_recv.at[d], (g, xx * y_n + y_peer(d)))
        copy.start()
        y_copies.append(copy)

    def key_copy(c, t):
        cols = pl.ds(aligned(t * TILE, TILE), TILE)
        return remote(kv.at[c, :, pl.ds(rows, rows), cols], kv.at[c, :, pl.ds(0, rows), cols],
                      key_send.at[c, t], key_recv.at[c, t], next_id)

    def query_copy(c, t):
        cols = pl.ds(aligned(t * TILE, TILE), TILE)
        return remote(qc.at[c, :, :, cols], qn.at[c, :, :, cols],
                      query_send.at[c, t], query_recv.at[c, t], prev_id)

    for copy in loads[2:4] + loads[6:8]:
        copy.wait()

    def start_raw(c, first, last):
        for t in range(first, last):
            key_copy(c, t).start()
            query_copy(c, t).start()

    start_raw(0, 0, 2)

    def fill_constants():
        for c in range(HALVES):
            own[c] = jnp.zeros(own.shape[1:], F32)
            mid_part[c] = jnp.zeros(mid_part.shape[1:], BF16)
            far_part[c] = jnp.zeros(far_part.shape[1:], BF16)
        bias[0:rows, :] = jnp.full((rows, rows), jnp.where(block > 0, 0.0, FLOOR), F32)
        key_row = lax.broadcasted_iota(jnp.int32, (rows, rows), 0)
        query_col = lax.broadcasted_iota(jnp.int32, (rows, rows), 1)
        bias[rows : 2 * rows, :] = jnp.where(key_row <= query_col, 0.0, FLOOR)
        mid_row = lax.broadcasted_iota(jnp.int32, (mid_rows, rows), 0)
        bias[mid_at : mid_at + mid_rows, :] = jnp.where(mid_row < m * coarse, 0.0, FLOOR)
        far_row = lax.broadcasted_iota(jnp.int32, (half, rows), 0)
        limit = jnp.minimum(g * n_seq, block - 1)
        for side in range(2):
            far_block = (2 * (far_row // n_seq) + side) * n_seq + far_row % n_seq
            at = far_at + side * half
            bias[at : at + half, :] = jnp.where(far_block < limit, 0.0, FLOOR)

    def far_slot(which):
        return pl.ds(aligned(far_at + core * half + which * n_seq, n_seq), n_seq)

    def far_copy(c, i, which, device):
        spot = kv.at[c, :, far_slot(which), :]
        return remote(spot, spot, z_send.at[c, i], z_recv.at[c, i], device)

    def start_far(c):
        def send(i, carry):
            far_copy(c, i, zz, (2 * z_peer(i) + core, m)).start()
            return carry

        lax.fori_loop(1, z_n, send, 0)

    def row_arrived(i, carry):
        row_copy(i, (m + n_seq - i) % n_seq, (g, m)).wait_recv()
        return carry

    lax.fori_loop(1, n_seq, row_arrived, 0)
    for c in range(HALVES):
        for kind in range(2):
            for t in range(tiles):
                lines = far_all[pl.ds(c * 16 + kind * 8 + t, n_seq, stride=32), :]
                kv[c, kind, far_slot(zz), t * TILE : (t + 1) * TILE] = lines.astype(BF16)
    start_far(0)

    for d in range(1, y_n):
        source = mid_slot(xx * y_n + (yy + y_n - d) % y_n, 1)
        spot = kv.at[:, :, source, :]
        remote(spot, spot, y_send.at[d], y_recv.at[d], (g, m)).wait_recv()
    x_copies = []
    for c in range(HALVES):
        for d in range(1, x_n):
            spot = kv.at[c, :, mid_slot(xx * y_n, y_n), :]
            copy = remote(spot, spot, x_send.at[c, d], x_recv.at[c, d], (g, x_peer(d) * y_n + yy))
            copy.start()
            x_copies.append(copy)
    start_raw(0, 2, tiles)
    fill_constants()

    def mid_ready(c):
        for d in range(1, x_n):
            spot = kv.at[c, :, mid_slot((xx + x_n - d) % x_n * y_n, y_n), :]
            remote(spot, spot, x_send.at[c, d], x_recv.at[c, d], (g, m)).wait_recv()

    def pair_copy(c):
        spot = kv.at[c, :, pl.ds(aligned(far_at + core * half, half), half), :]
        return remote(spot, spot, pair_send.at[c], pair_recv.at[c], twin_id)

    def forward_far(c):
        def arrived(i, carry):
            far_copy(c, i, (zz + z_n - i) % z_n, (g, m)).wait_recv()
            return carry

        lax.fori_loop(1, z_n, arrived, 0)
        pair_copy(c).start()

    def far_ready(c):
        spot = kv.at[c, :, pl.ds(aligned(far_at + (1 - core) * half, half), half), :]
        remote(spot, spot, pair_send.at[c], pair_recv.at[c], (g, m)).wait_recv()

    total = far_at + n_far

    def head_window(j):
        tile = jnp.maximum((j * depth + depth - 1) // TILE - 1, 0)
        start = aligned(tile * TILE, TILE)
        lane = lax.broadcasted_iota(jnp.int32, (8, WINDOW), 1) + start
        inside = (lane >= j * depth) & (lane < j * depth + depth)
        keep = jnp.where(inside, 1.0, 0.0)[0:1, :]
        return pl.ds(start, WINDOW), keep, j * depth - start

    def only(loaded, keep):
        return (loaded.astype(F32) * keep).astype(BF16)

    def pad_head(u, j, kind, offset):
        padded[u, kind] = jnp.zeros((WINDOW, rows), BF16)
        padded[u, kind, pl.ds(aligned(offset, 16), depth), :] = qc_t[
            kind, pl.ds(aligned(j * depth, depth), depth), :
        ]
        return padded[u, kind]

    def main(c):
        for kind in range(2):
            kvt[kind, :, rows:total] = kv[c, kind, rows:total, :].T
            qc_t[kind] = qc[c, kind].T

        def arrive(t):
            key_copy(c, t).wait_recv()
            cols = pl.ds(aligned(t * TILE, TILE), TILE)
            for kind in range(2):
                kvt[kind, cols, 0:rows] = kv[c, kind, 0:rows, cols].T

        arrive(0)

        def step(i, carry):
            if c == 0:
                @pl.when(i == 2)
                def _():
                    forward_far(1)
            else:
                @pl.when(i == 1)
                def _():
                    send_far(0, 1)

            @pl.when(i == 2)
            def _():
                core_copy(c, 0).start()

            @pl.when(i == 3)
            def _():
                send_far(c, 0)

            arrive(i + 1)
            js = [i * PAIR + u for u in range(PAIR)]
            windows, queries, cots, cots_t, tops = [], [], [], [], []
            for u, j in enumerate(js):
                window, keep, offset = head_window(j)
                windows.append(window)
                queries.append(only(qc[c, 0, :, window], keep))
                cots.append(only(qc[c, 1, :, window], keep))
                cots_t.append(pad_head(u, j, 1, offset))
                s = dot(kv[c, 0, :, window], pad_head(u, j, 0, offset)) + bias[...]
                score[u] = s
                tops.append(jnp.max(s, axis=0, keepdims=True) * to_log2)
            inverses, deltas = [], []
            for u, j in enumerate(js):
                e = jnp.exp2(score[u] * to_log2 - tops[u])
                score[u] = e
                norm = jnp.sum(e, axis=0, keepdims=True)
                inverse = 1.0 / norm
                weight[u] = (score[u] * inverse).astype(BF16)
                inverses.append(inverse)
                head_rows = pl.ds(aligned(j * depth, depth), depth)
                mixed = dot(kvt[1, head_rows, :], weight[u]).astype(BF16)
                out_t[head_rows, :] = mixed
                delta = jnp.sum(
                    qc_t[1, head_rows, :].astype(F32) * mixed.astype(F32), axis=0, keepdims=True
                )
                deltas.append(delta)
                stat[c, pl.ds(j, 1), :] = tops[u] + jnp.log(norm) * LOG2E
                stat[c, pl.ds(heads + j, 1), :] = delta
            for u, j in enumerate(js):
                dprob = dot(kv[c, 1, :, windows[u]], cots_t[u])
                dscore[u] = (score[u] * ((dprob - deltas[u]) * inverses[u])).astype(BF16)
                head_rows = pl.ds(aligned(j * depth, depth), depth)
                dq_t[head_rows, :] = (dot(kvt[0, head_rows, :], dscore[u]) * scale).astype(BF16)
                for kind, (left, right) in enumerate(((dscore, queries[u]), (weight, cots[u]))):
                    grad = dot(left[u, rows:total, :], right)
                    own[c, kind, :, windows[u]] += grad[0:rows]
                    mid_part[c, kind, :, windows[u]] += grad[rows : rows + mid_rows].astype(BF16)
                    far_part[c, kind, :, windows[u]] += grad[rows + mid_rows :].astype(BF16)
            return carry

        lax.fori_loop(0, heads // PAIR, step, 0)

    def stat_copy(c):
        return remote(stat.at[c], stat_next.at[c], stat_send.at[c], stat_recv.at[c], prev_id)

    def store(c, kind, src, ref):
        return pltpu.make_async_copy(src, ref.at[:, pl.ds(c * part, part)], store_sem.at[c * 4 + kind])

    def piece(p):
        return pl.ds(0, 2 * TILE) if p == 0 else pl.ds(2 * TILE, part - 2 * TILE)

    def core_copy(c, p):
        src = far_part.at[c, :, pl.ds(aligned((1 - core) * half, half), half), piece(p)]
        return remote(src, core_in.at[c, :, :, piece(p)], core_send.at[c, p], core_recv.at[c, p], twin_id)

    def mid_x_copy(c, d):
        src = mid_part.at[c, :, pl.ds(aligned(x_peer(d) * y_n * coarse, coarse), y_n * coarse), :]
        return remote(src, mid_x_in.at[c, d - 1], mx_send.at[c, d], mx_recv.at[c, d],
                      (g, x_peer(d) * y_n + yy))

    def mid_y_copy(c, d):
        src = mid_x.at[c, :, pl.ds(aligned(y_peer(d) * coarse, coarse), coarse), :]
        return remote(src, mid_y_in.at[c, d - 1], my_send.at[c, d], my_recv.at[c, d],
                      (g, xx * y_n + y_peer(d)))

    def far_z_copy(c, p, i):
        src = core_sum.at[c, :, pl.ds(aligned(z_peer(i) * n_seq, n_seq), n_seq), piece(p)]
        return remote(src, far_in.at[c, i, :, :, piece(p)], fz_send.at[c, p, i], fz_recv.at[c, p, i],
                      (2 * z_peer(i) + core, m))

    def far_row_copy(c, i):
        member = (m + i) % n_seq
        src = far_rows.at[c, pl.ds(aligned(member * 16, 16), 16), :]
        dst = far_rows_in.at[c, pl.ds(aligned(i * 16, 16), 16), :]
        return remote(src, dst, fs_send.at[c, i], fs_recv.at[c, i], (g, member))

    def send_parts(c):
        core_copy(c, 1).start()
        stat_copy(c).start()
        for d in range(1, x_n):
            mid_x_copy(c, d).start()
        out_rows[c, 0] = out_t[...].T
        out_rows[c, 1] = dq_t[...].T
        store(c, 0, out_rows.at[c, 0], o_hbm).start()
        store(c, 1, out_rows.at[c, 1], dq_hbm).start()

    def send_far(c, p):
        core_copy(c, p).wait_recv()
        mine = pl.ds(aligned(core * half, half), half)
        for kind in range(2):
            both = far_part[c, kind, mine, piece(p)].astype(F32) + core_in[c, kind, :, piece(p)].astype(F32)
            core_sum[c, kind, :, piece(p)] = both.astype(BF16)

        def send(i, carry):
            far_z_copy(c, p, i).start()
            return carry

        lax.fori_loop(1, z_n, send, 0)

    def send_mid(c):
        for d in range(1, x_n):
            mid_x_copy(c, d).wait_recv()
        mine = pl.ds(aligned(xx * y_n * coarse, coarse), y_n * coarse)
        for kind in range(2):
            added = mid_part[c, kind, mine, :].astype(F32)
            for d in range(1, x_n):
                added = added + mid_x_in[c, d - 1, kind].astype(F32)
            mid_x[c, kind] = added.astype(BF16)
        for d in range(1, y_n):
            mid_y_copy(c, d).start()

    def send_rows(c):
        def arrived(i, carry):
            far_z_copy(c, 0, i).wait_recv()
            far_z_copy(c, 1, i).wait_recv()
            return carry

        lax.fori_loop(1, z_n, arrived, 0)
        mine = pl.ds(aligned(zz * n_seq, n_seq), n_seq)
        for kind in range(2):
            def add(i, added, kind=kind):
                return added + far_in[c, i, kind].astype(F32)

            added = lax.fori_loop(1, z_n, add, core_sum[c, kind, mine, :].astype(F32))
            for t in range(tiles):
                far_rows[c, pl.ds(kind * 8 + t, n_seq, stride=16), :] = added[:, t * TILE : (t + 1) * TILE]

        def send(i, carry):
            far_row_copy(c, i).start()
            return carry

        lax.fori_loop(1, n_seq, send, 0)
        far_rows_in[c, 0:16, :] = far_rows[c, pl.ds(aligned(m * 16, 16), 16), :]

    def from_next(c):
        for t in range(tiles):
            query_copy(c, t).wait_recv()
        stat_copy(c).wait_recv()
        for kind in range(2):
            qc_t[kind] = qn[c, kind].T
        there = block < n_blocks - 1

        def step(i, carry):
            for u in range(PAIR):
                j = i * PAIR + u
                window, keep, offset = head_window(j)
                query = only(qn[c, 0, :, window], keep)
                cot = only(qn[c, 1, :, window], keep)
                s = dot(kv[c, 0, rows : 2 * rows, window], pad_head(u, j, 0, offset))
                s = jnp.where(there, s, FLOOR)
                p = jnp.exp2(s * to_log2 - stat_next[c, pl.ds(j, 1), :])
                dprob = dot(kv[c, 1, rows : 2 * rows, window], pad_head(u, j, 1, offset))
                ds = (p * (dprob - stat_next[c, pl.ds(heads + j, 1), :])).astype(BF16)
                own[c, 0, :, window] += dot(ds, query)
                own[c, 1, :, window] += dot(p.astype(BF16), cot)
            return carry

        lax.fori_loop(0, heads // PAIR, step, 0)

    def finish(c):
        for d in range(1, y_n):
            mid_y_copy(c, d).wait_recv()

        def arrived(i, carry):
            far_row_copy(c, i).wait_recv()
            return carry

        lax.fori_loop(1, n_seq, arrived, 0)
        far_sum = far_rows_in[c, 0:16, :]
        for i in range(1, n_seq):
            far_sum = far_sum + far_rows_in[c, i * 16 : (i + 1) * 16, :]
        mine = pl.ds(aligned(yy * coarse, coarse), coarse)
        for kind in range(2):
            factor = scale if kind == 0 else 1.0
            added = mid_x[c, kind, mine, :].astype(F32)
            for d in range(1, y_n):
                added = added + mid_y_in[c, d - 1, kind].astype(F32)
            for t in range(tiles):
                cols = slice(t * TILE, (t + 1) * TILE)
                far = far_sum[kind * 8 + t : kind * 8 + t + 1, :] / math.sqrt(coarse)
                spread = (added[:, cols] + far) * (factor / math.sqrt(POOL))
                for i in range(coarse):
                    raw = own[c, kind, i * POOL : (i + 1) * POOL, cols] * factor
                    grad_rows[c, kind, i * POOL : (i + 1) * POOL, cols] = (
                        raw + spread[i : i + 1, :]
                    ).astype(BF16)
        store(c, 2, grad_rows.at[c, 0], dk_hbm).start()
        store(c, 3, grad_rows.at[c, 1], dv_hbm).start()

    forward_far(0)
    start_far(1)
    start_raw(1, 0, tiles)
    mid_ready(0)
    far_ready(0)
    main(0)
    send_parts(0)
    mid_ready(1)
    far_ready(1)
    main(1)
    send_parts(1)
    send_mid(0)
    send_far(1, 1)
    from_next(0)
    send_rows(0)
    send_mid(1)
    from_next(1)
    finish(0)
    send_rows(1)
    finish(1)

    for copy in y_copies + x_copies:
        copy.wait_send()
    for c in range(HALVES):
        for t in range(tiles):
            key_copy(c, t).wait_send()
            query_copy(c, t).wait_send()
        pair_copy(c).wait_send()
        stat_copy(c).wait_send()
        core_copy(c, 0).wait_send()
        core_copy(c, 1).wait_send()
        for d in range(1, x_n):
            mid_x_copy(c, d).wait_send()
        for d in range(1, y_n):
            mid_y_copy(c, d).wait_send()

        def left_z(i, carry, c=c):
            far_copy(c, i, zz, (2 * z_peer(i) + core, m)).wait_send()
            far_z_copy(c, 0, i).wait_send()
            far_z_copy(c, 1, i).wait_send()
            return carry

        def left_rows(i, carry, c=c):
            far_row_copy(c, i).wait_send()
            if c == 0:
                row_copy(i, m, (g, (m + i) % n_seq)).wait_send()
            return carry

        lax.fori_loop(1, z_n, left_z, 0)
        lax.fori_loop(1, n_seq, left_rows, 0)
        store(c, 0, out_rows.at[c, 0], o_hbm).wait()
        store(c, 1, out_rows.at[c, 1], dq_hbm).wait()
        store(c, 2, grad_rows.at[c, 0], dk_hbm).wait()
        store(c, 3, grad_rows.at[c, 1], dv_hbm).wait()


def hand_over(a, b, c, d, to_a, to_b, to_c, to_d):
    for src, dst in ((a, to_a), (b, to_b), (c, to_c), (d, to_d)):
        dst[...] = src[...]


def body(query, keys, values, cotangent):
    rows, width = query.shape
    n_seq = lax.axis_size("seq")
    n_grp = lax.axis_size("grp")
    part = width // HALVES
    coarse = rows // POOL
    mid_rows = n_seq * coarse
    n_far = n_grp * n_seq
    half = n_far // 2
    total = 2 * rows + mid_rows + n_far
    y_n = math.isqrt(n_seq)
    x_n = n_seq // y_n
    z_n = n_grp // 2
    heads = HEADS // HALVES
    tiles = part // TILE
    vmem = pltpu.VMEM
    dma = pltpu.SemaphoreType.DMA
    scratch = [
        vmem((HALVES, 2, total, part), BF16),
        vmem((HALVES, 2, rows, part), BF16),
        vmem((HALVES, 2, rows, part), BF16),
        vmem((2, part, total), BF16),
        vmem((2, part, rows), BF16),
        vmem((total, rows), F32),
        vmem((PAIR, total, rows), F32),
        vmem((PAIR, total, rows), BF16),
        vmem((PAIR, total, rows), BF16),
        vmem((part, rows), BF16),
        vmem((part, rows), BF16),
        vmem((HALVES, 2, rows, part), BF16),
        vmem((HALVES, 2 * heads, rows), F32),
        vmem((HALVES, 2 * heads, rows), F32),
        vmem((HALVES, 2, rows, part), F32),
        vmem((HALVES, 2, mid_rows, part), BF16),
        vmem((HALVES, 2, n_far, part), BF16),
        vmem((HALVES, 2, half, part), BF16),
        vmem((HALVES, 2, half, part), BF16),
        vmem((HALVES, z_n, 2, n_seq, part), BF16),
        vmem((HALVES, n_seq * 16, TILE), F32),
        vmem((HALVES, n_seq * 16, TILE), F32),
        vmem((HALVES, x_n - 1, 2, y_n * coarse, part), BF16),
        vmem((HALVES, 2, y_n * coarse, part), BF16),
        vmem((HALVES, y_n - 1, 2, coarse, part), BF16),
        vmem((HALVES, 2, rows, part), BF16),
        vmem((32, TILE), F32),
        vmem((n_seq * 32, TILE), F32),
        vmem((PAIR, 2, WINDOW, rows), BF16),
        dma((HALVES * 4,)),
        dma((n_seq,)), dma((n_seq,)),
        dma((y_n,)), dma((y_n,)),
        dma((HALVES, tiles)), dma((HALVES, tiles)),
        dma((HALVES, tiles)), dma((HALVES, tiles)),
        dma((HALVES, x_n)), dma((HALVES, x_n)),
        dma((HALVES, z_n)), dma((HALVES, z_n)),
        dma((HALVES,)), dma((HALVES,)),
        dma((HALVES,)), dma((HALVES,)),
        dma((HALVES, 2)), dma((HALVES, 2)),
        dma((HALVES, x_n)), dma((HALVES, x_n)),
        dma((HALVES, y_n)), dma((HALVES, y_n)),
        dma((HALVES, 2, z_n)), dma((HALVES, 2, z_n)),
        dma((HALVES, n_seq)), dma((HALVES, n_seq)),
        dma((HALVES * 4,)),
    ]
    flops = 12 * rows * total * width
    results = pl.pallas_call(
        functools.partial(kernel, n_grp, n_seq),
        out_shape=[jax.ShapeDtypeStruct((rows, width), BF16)] * 4,
        in_specs=[pl.BlockSpec(memory_space=pl.ANY)] * 4,
        out_specs=[pl.BlockSpec(memory_space=pl.ANY)] * 4,
        scratch_shapes=scratch,
        compiler_params=pltpu.CompilerParams(
            collective_id=0, has_side_effects=True, vmem_limit_bytes=60 * 2**20
        ),
        cost_estimate=pl.CostEstimate(
            flops=flops, bytes_accessed=16 * rows * width, transcendentals=HEADS * rows * total
        ),
    )(query, keys, values, cotangent)
    block = pl.BlockSpec((rows // 4, width), lambda i: (i, 0))
    return pl.pallas_call(
        hand_over,
        grid=(4,),
        out_shape=[jax.ShapeDtypeStruct((rows, width), BF16)] * 4,
        in_specs=[block] * 4,
        out_specs=[block] * 4,
        cost_estimate=pl.CostEstimate(flops=0, bytes_accessed=16 * rows * width, transcendentals=0),
        compiler_params=pltpu.CompilerParams(vmem_limit_bytes=60 * 2**20),
    )(*results)


def solution(mesh):
    spec = P(("grp", "seq"), None)
    return jax.shard_map(
        body, mesh=mesh, in_specs=(spec,) * 4, out_specs=(spec,) * 4, check_vma=False
    )
```

```python
import functools
import math

import jax
import jax.numpy as jnp
from jax import lax
from jax.experimental import pallas as pl
from jax.experimental.pallas import tpu as pltpu
from jax.sharding import PartitionSpec as P

HEADS = 16
POOL = 16
HALVES = 2
TILE = 128
WINDOW = 256
PAIR = 2
FLOOR = -1e30
LOG2E = 1.4426950408889634
MESH = pl.DeviceIdType.MESH
F32 = jnp.float32
BF16 = jnp.bfloat16


def dot(a, b):
    return jnp.dot(a, b, preferred_element_type=F32)


def kernel(
    n_grp, n_seq,
    q_hbm, k_hbm, v_hbm, c_hbm,
    o_hbm, dq_hbm, dk_hbm, dv_hbm,
    kv, qc, qn, kvt, qc_t, bias, score, weight, dscore,
    out_t, dq_t, out_rows, stat, stat_next, own, mid_part, far_part,
    core_in, core_sum, far_in, far_rows, far_rows_in,
    mid_x_in, mid_x, mid_y_in, grad_rows, far_mine, far_all, padded, cross_out, cross_in, z_sum, mine_z,
    load_sem, across_send, across_recv, cross_send, cross_recv, row_send, row_recv, y_send, y_recv, key_send, key_recv, query_send, query_recv, x_send, x_recv, z_send, z_recv,
    pair_send, pair_recv, stat_send, stat_recv, core_send, core_recv,
    mx_send, mx_recv, my_send, my_recv, fz_send, fz_recv, fs_send, fs_recv, store_sem,
):
    rows = q_hbm.shape[0]
    width = q_hbm.shape[1]
    part = width // HALVES
    heads = HEADS // HALVES
    depth = width // HEADS
    coarse = rows // POOL
    mid_rows = n_seq * coarse
    n_far = n_grp * n_seq
    half = n_far // 2
    y_n = math.isqrt(n_seq)
    x_n = n_seq // y_n
    z_n = n_grp // 4
    mid_at = 2 * rows
    far_at = mid_at + mid_rows
    scale = 1.0 / math.sqrt(depth)
    to_log2 = scale * LOG2E
    tiles = part // TILE

    g = lax.axis_index("grp")
    m = lax.axis_index("seq")
    core = g % 2
    side_y = g // 2 // z_n
    zz = g // 2 % z_n
    xx = m // y_n
    yy = m % y_n
    block = g * n_seq + m
    n_blocks = n_grp * n_seq
    after = (block + 1) % n_blocks
    before = (block + n_blocks - 1) % n_blocks
    next_id = (after // n_seq, after % n_seq)
    prev_id = (before // n_seq, before % n_seq)
    twin_id = (g + 1 - 2 * core, m)
    across_id = (2 * ((1 - side_y) * z_n + zz) + core, m)

    def y_peer(d):
        return (yy + d) % y_n

    def x_peer(d):
        return (xx + d) % x_n

    def z_peer(i):
        return (zz + i) % z_n

    def z_id(i):
        return (2 * (side_y * z_n + z_peer(i)) + core, m)

    def remote(src, dst, send, recv, device):
        return pltpu.make_async_remote_copy(
            src_ref=src, dst_ref=dst, send_sem=send, recv_sem=recv,
            device_id=device, device_id_type=MESH,
        )

    def aligned(start, unit):
        return pl.multiple_of(start, unit)

    loads = []
    for c in range(HALVES):
        cols = pl.ds(c * part, part)
        for kind, (ref, dst) in enumerate((
            (k_hbm, kv.at[c, 0, pl.ds(rows, rows)]), (v_hbm, kv.at[c, 1, pl.ds(rows, rows)]),
            (q_hbm, qc.at[c, 0]), (c_hbm, qc.at[c, 1]),
        )):
            loads.append(pltpu.make_async_copy(ref.at[:, cols], dst, load_sem.at[c * 4 + kind]))
    for copy in loads:
        copy.start()

    barrier = pltpu.get_barrier_semaphore()

    def greet(device):
        pl.semaphore_signal(barrier, inc=1, device_id=device, device_id_type=MESH)

    def greet_seq(i, carry):
        greet((g, (m + i) % n_seq))
        return carry

    def greet_z(i, carry):
        greet(z_id(i))
        return carry

    lax.fori_loop(1, n_seq, greet_seq, 0)
    lax.fori_loop(1, z_n, greet_z, 0)
    greet(twin_id)
    greet(across_id)
    greet(next_id)
    greet(prev_id)

    for c in range(HALVES):
        for kind in range(2):
            loads[c * 4 + kind].wait()

    def pooling(n, count):
        row = lax.broadcasted_iota(jnp.int32, (n, n * count), 0)
        col = lax.broadcasted_iota(jnp.int32, (n, n * count), 1)
        return jnp.where((col >= row * count) & (col < row * count + count), 1.0, 0.0).astype(BF16)

    own_mid = pl.ds(aligned(mid_at + m * coarse, coarse), coarse)
    pool_mid = pooling(coarse, POOL)
    for c in range(HALVES):
        for kind in range(2):
            summed = dot(pool_mid, kv[c, kind, rows : 2 * rows, :])
            pooled = (summed / math.sqrt(POOL)).astype(BF16)
            kv[c, kind, own_mid, :] = pooled
            row = jnp.sum(pooled.astype(F32), axis=0, keepdims=True) / math.sqrt(coarse)
            row = row.astype(BF16).astype(F32)
            for t in range(tiles):
                at = c * 16 + kind * 8 + t
                far_mine[at : at + 1, :] = row[:, t * TILE : (t + 1) * TILE]

    pl.semaphore_wait(barrier, (n_seq - 1) + (z_n - 1) + 4)

    def row_copy(i, source, device):
        spot = far_all.at[pl.ds(aligned(source * 32, 32), 32), :]
        return remote(far_mine, spot, row_send.at[i], row_recv.at[i], device)

    def send_row(i, carry):
        row_copy(i, m, (g, (m + i) % n_seq)).start()
        return carry

    lax.fori_loop(1, n_seq, send_row, 0)
    far_all[pl.ds(aligned(m * 32, 32), 32), :] = far_mine[...]

    def mid_slot(member_start, count):
        return pl.ds(aligned(mid_at + member_start * coarse, coarse), count * coarse)

    y_copies = []
    for d in range(1, y_n):
        spot = kv.at[:, :, own_mid, :]
        copy = remote(spot, spot, y_send.at[d], y_recv.at[d], (g, xx * y_n + y_peer(d)))
        copy.start()
        y_copies.append(copy)

    def key_copy(c, t):
        cols = pl.ds(aligned(t * TILE, TILE), TILE)
        return remote(kv.at[c, :, pl.ds(rows, rows), cols], kv.at[c, :, pl.ds(0, rows), cols],
                      key_send.at[c, t], key_recv.at[c, t], next_id)

    def query_copy(c, t):
        cols = pl.ds(aligned(t * TILE, TILE), TILE)
        return remote(qc.at[c, :, :, cols], qn.at[c, :, :, cols],
                      query_send.at[c, t], query_recv.at[c, t], prev_id)

    for copy in loads[2:4] + loads[6:8]:
        copy.wait()

    def start_raw(c, first, last):
        for t in range(first, last):
            key_copy(c, t).start()
            query_copy(c, t).start()

    start_raw(0, 0, 2)

    def fill_constants():
        for c in range(HALVES):
            own[c] = jnp.zeros(own.shape[1:], F32)
            mid_part[c] = jnp.zeros(mid_part.shape[1:], BF16)
            far_part[c] = jnp.zeros(far_part.shape[1:], BF16)
        bias[0:rows, :] = jnp.full((rows, rows), jnp.where(block > 0, 0.0, FLOOR), F32)
        key_row = lax.broadcasted_iota(jnp.int32, (rows, rows), 0)
        query_col = lax.broadcasted_iota(jnp.int32, (rows, rows), 1)
        bias[rows : 2 * rows, :] = jnp.where(key_row <= query_col, 0.0, FLOOR)
        mid_row = lax.broadcasted_iota(jnp.int32, (mid_rows, rows), 0)
        bias[mid_at : mid_at + mid_rows, :] = jnp.where(mid_row < m * coarse, 0.0, FLOOR)
        far_row = lax.broadcasted_iota(jnp.int32, (half, rows), 0)
        limit = jnp.minimum(g * n_seq, block - 1)
        for side in range(2):
            chip = far_row // n_seq % 2 * z_n + far_row // (2 * n_seq)
            far_block = (2 * chip + side) * n_seq + far_row % n_seq
            at = far_at + side * half
            bias[at : at + half, :] = jnp.where(far_block < limit, 0.0, FLOOR)

    def far_slot(which_z, which_y, count):
        at = far_at + core * half + (2 * which_z + which_y) * n_seq
        return pl.ds(aligned(at, n_seq), count * n_seq)

    def across_copy(which_y):
        spot = kv.at[:, :, far_slot(zz, which_y, 1), :]
        return remote(spot, spot, across_send.at[0], across_recv.at[0], across_id)

    def far_copy(c, i, which, device):
        spot = kv.at[c, :, far_slot(which, 0, 2), :]
        return remote(spot, spot, z_send.at[c, i], z_recv.at[c, i], device)

    def start_far(c):
        def send(i, carry):
            far_copy(c, i, zz, z_id(i)).start()
            return carry

        lax.fori_loop(1, z_n, send, 0)

    def row_arrived(i, carry):
        row_copy(i, (m + n_seq - i) % n_seq, (g, m)).wait_recv()
        return carry

    lax.fori_loop(1, n_seq, row_arrived, 0)
    for c in range(HALVES):
        for kind in range(2):
            for t in range(tiles):
                lines = far_all[pl.ds(c * 16 + kind * 8 + t, n_seq, stride=32), :]
                kv[c, kind, far_slot(zz, side_y, 1), t * TILE : (t + 1) * TILE] = lines.astype(BF16)
    across_copy(side_y).start()

    for d in range(1, y_n):
        source = mid_slot(xx * y_n + (yy + y_n - d) % y_n, 1)
        spot = kv.at[:, :, source, :]
        remote(spot, spot, y_send.at[d], y_recv.at[d], (g, m)).wait_recv()
    x_copies = []
    for c in range(HALVES):
        for d in range(1, x_n):
            spot = kv.at[c, :, mid_slot(xx * y_n, y_n), :]
            copy = remote(spot, spot, x_send.at[c, d], x_recv.at[c, d], (g, x_peer(d) * y_n + yy))
            copy.start()
            x_copies.append(copy)
    across_copy(1 - side_y).wait_recv()
    start_far(0)
    start_raw(0, 2, 3)
    fill_constants()

    def mid_ready(c):
        for d in range(1, x_n):
            spot = kv.at[c, :, mid_slot((xx + x_n - d) % x_n * y_n, y_n), :]
            remote(spot, spot, x_send.at[c, d], x_recv.at[c, d], (g, m)).wait_recv()

    def pair_copy(c):
        spot = kv.at[c, :, pl.ds(aligned(far_at + core * half, half), half), :]
        return remote(spot, spot, pair_send.at[c], pair_recv.at[c], twin_id)

    def forward_far(c):
        def arrived(i, carry):
            far_copy(c, i, (zz + z_n - i) % z_n, (g, m)).wait_recv()
            return carry

        lax.fori_loop(1, z_n, arrived, 0)
        pair_copy(c).start()

    def far_ready(c):
        spot = kv.at[c, :, pl.ds(aligned(far_at + (1 - core) * half, half), half), :]
        remote(spot, spot, pair_send.at[c], pair_recv.at[c], (g, m)).wait_recv()

    total = far_at + n_far

    wide = PAIR * rows

    def pair_window(i):
        return aligned(i * PAIR * depth // TILE * TILE, TILE)

    def head_rows(j):
        return pl.ds(aligned(j * depth, depth), depth)

    def pad_heads(i, kind):
        padded[kind] = jnp.zeros((WINDOW, wide), BF16)
        for u in range(PAIR):
            j = i * PAIR + u
            at = pl.ds(aligned(j * depth - pair_window(i), 16), depth)
            padded[kind, at, u * rows : (u + 1) * rows] = qc_t[kind, head_rows(j), :]

    def stacked(loaded, i):
        lane = lax.broadcasted_iota(jnp.int32, (8, WINDOW), 1) + pair_window(i)
        heads_of = []
        for u in range(PAIR):
            at = (i * PAIR + u) * depth
            keep = jnp.where((lane >= at) & (lane < at + depth), 1.0, 0.0)[0:1, :]
            heads_of.append((loaded.astype(F32) * keep).astype(BF16))
        return jnp.concatenate(heads_of, axis=0)

    def prepare(c, at, size):
        for kind in range(2):
            kvt[kind, :, at : at + size] = kv[c, kind, at : at + size, :].T

    def prepare_own(c):
        for kind in range(2):
            qc_t[kind] = qc[c, kind].T
        prepare(c, rows, rows)

    def main(c):
        def arrive(t):
            key_copy(c, t).wait_recv()
            cols = pl.ds(aligned(t * TILE, TILE), TILE)
            for kind in range(2):
                kvt[kind, cols, 0:rows] = kv[c, kind, 0:rows, cols].T

        arrive(0)

        def step(i, carry):
            if c == 0:
                key_copy(1, i).start()
                query_copy(1, i).start()

                @pl.when(i == 3)
                def _():
                    forward_far(1)
            else:
                @pl.when(i == 2)
                def _():
                    send_far(0, 0)
                    send_far(0, 1)

            @pl.when(i == 2)
            def _():
                core_copy(c, 0).start()

            arrive(i + 1)
            window = pl.ds(pair_window(i), WINDOW)
            pad_heads(i, 0)
            pad_heads(i, 1)
            seen = bias[...]
            s = dot(kv[c, 0, :, window], padded[0]) + jnp.concatenate([seen] * PAIR, axis=1)
            score[...] = s
            top = jnp.max(s, axis=0, keepdims=True) * to_log2
            norm = jnp.zeros((1, wide), F32)
            for at in range(0, total, rows):
                e = jnp.exp2(score[at : at + rows, :] * to_log2 - top)
                score[at : at + rows, :] = e
                norm = norm + jnp.sum(e, axis=0, keepdims=True)
            inverse = 1.0 / norm
            for at in range(0, total, rows):
                weight[at : at + rows, :] = (score[at : at + rows, :] * inverse).astype(BF16)
            log_norm = top + jnp.log(norm) * LOG2E
            deltas = []
            for u in range(PAIR):
                j = i * PAIR + u
                own_cols = slice(u * rows, (u + 1) * rows)
                mixed = dot(kvt[1, head_rows(j), :], weight[:, own_cols]).astype(BF16)
                out_t[head_rows(j), :] = mixed
                delta = jnp.sum(
                    qc_t[1, head_rows(j), :].astype(F32) * mixed.astype(F32), axis=0, keepdims=True
                )
                deltas.append(delta)
                stat[c, pl.ds(j, 1), :] = log_norm[:, own_cols]
                stat[c, pl.ds(heads + j, 1), :] = delta
            delta = jnp.concatenate(deltas, axis=1)
            dprob = dot(kv[c, 1, :, window], padded[1])
            dscore[...] = (score[...] * ((dprob - delta) * inverse)).astype(BF16)
            for u in range(PAIR):
                j = i * PAIR + u
                mixed = dot(kvt[0, head_rows(j), :], dscore[:, u * rows : (u + 1) * rows])
                dq_t[head_rows(j), :] = (mixed * scale).astype(BF16)
            for kind, left in enumerate((dscore, weight)):
                grad = dot(left[rows:total, :], stacked(qc[c, kind, :, window], i))
                own[c, kind, :, window] += grad[0:rows]
                mid_part[c, kind, :, window] += grad[rows : rows + mid_rows].astype(BF16)
                far_part[c, kind, :, window] += grad[rows + mid_rows :].astype(BF16)
            return carry

        lax.fori_loop(0, heads // PAIR, step, 0)

    def stat_copy(c):
        return remote(stat.at[c], stat_next.at[c], stat_send.at[c], stat_recv.at[c], prev_id)

    def store(c, kind, src, ref):
        return pltpu.make_async_copy(src, ref.at[:, pl.ds(c * part, part)], store_sem.at[c * 4 + kind])

    def piece(p):
        return pl.ds(0, 2 * TILE) if p == 0 else pl.ds(2 * TILE, part - 2 * TILE)

    def core_copy(c, p):
        src = far_part.at[c, :, pl.ds(aligned((1 - core) * half, half), half), piece(p)]
        return remote(src, core_in.at[c, :, :, piece(p)], core_send.at[c, p], core_recv.at[c, p], twin_id)

    def mid_x_copy(c, d):
        src = mid_part.at[c, :, pl.ds(aligned(x_peer(d) * y_n * coarse, coarse), y_n * coarse), :]
        return remote(src, mid_x_in.at[c, d - 1], mx_send.at[c, d], mx_recv.at[c, d],
                      (g, x_peer(d) * y_n + yy))

    def mid_y_copy(c, d):
        src = mid_x.at[c, :, pl.ds(aligned(y_peer(d) * coarse, coarse), coarse), :]
        return remote(src, mid_y_in.at[c, d - 1], my_send.at[c, d], my_recv.at[c, d],
                      (g, xx * y_n + y_peer(d)))

    def far_z_copy(c, p, i):
        src = core_sum.at[c, :, pl.ds(aligned(z_peer(i) * 2 * n_seq, 2 * n_seq), 2 * n_seq), piece(p)]
        return remote(src, far_in.at[c, i, :, :, piece(p)], fz_send.at[c, p, i], fz_recv.at[c, p, i],
                      z_id(i))

    def cross_copy(c):
        return remote(cross_out.at[c], cross_in.at[c], cross_send.at[c], cross_recv.at[c], across_id)

    def far_row_copy(c, i):
        member = (m + i) % n_seq
        src = far_rows.at[c, pl.ds(aligned(member * 16, 16), 16), :]
        dst = far_rows_in.at[c, pl.ds(aligned(i * 16, 16), 16), :]
        return remote(src, dst, fs_send.at[c, i], fs_recv.at[c, i], (g, member))

    def send_parts(c):
        core_copy(c, 1).start()
        stat_copy(c).start()
        for d in range(1, x_n):
            mid_x_copy(c, d).start()
        out_rows[c, 0] = out_t[...].T
        out_rows[c, 1] = dq_t[...].T
        store(c, 0, out_rows.at[c, 0], o_hbm).start()
        store(c, 1, out_rows.at[c, 1], dq_hbm).start()

    def send_far(c, p):
        core_copy(c, p).wait_recv()
        mine = pl.ds(aligned(core * half, half), half)
        for kind in range(2):
            both = far_part[c, kind, mine, piece(p)].astype(F32) + core_in[c, kind, :, piece(p)].astype(F32)
            core_sum[c, kind, :, piece(p)] = both.astype(BF16)

        def send(i, carry):
            far_z_copy(c, p, i).start()
            return carry

        lax.fori_loop(1, z_n, send, 0)

    def send_mid(c):
        for d in range(1, x_n):
            mid_x_copy(c, d).wait_recv()
        mine = pl.ds(aligned(xx * y_n * coarse, coarse), y_n * coarse)
        for kind in range(2):
            added = mid_part[c, kind, mine, :].astype(F32)
            for d in range(1, x_n):
                added = added + mid_x_in[c, d - 1, kind].astype(F32)
            mid_x[c, kind] = added.astype(BF16)
        for d in range(1, y_n):
            mid_y_copy(c, d).start()

    def cross_far(c):
        def arrived(i, carry):
            far_z_copy(c, 0, i).wait_recv()
            far_z_copy(c, 1, i).wait_recv()
            return carry

        lax.fori_loop(1, z_n, arrived, 0)
        for which in range(2):
            at = aligned((2 * zz + which) * n_seq, n_seq)
            for kind in range(2):
                def add(i, added, kind=kind, which=which):
                    return added + far_in[c, i, kind, which * n_seq : (which + 1) * n_seq, :].astype(F32)

                added = core_sum[c, kind, pl.ds(at, n_seq), :].astype(F32)
                z_sum[which, kind] = lax.fori_loop(1, z_n, add, added)
        for kind in range(2):
            cross_out[c, kind] = z_sum[1 - side_y, kind]
            mine_z[c, kind] = z_sum[side_y, kind]
        cross_copy(c).start()

    def send_rows(c):
        cross_copy(c).wait_recv()
        for kind in range(2):
            added = mine_z[c, kind] + cross_in[c, kind]
            for t in range(tiles):
                far_rows[c, pl.ds(kind * 8 + t, n_seq, stride=16), :] = added[:, t * TILE : (t + 1) * TILE]

        def send(i, carry):
            far_row_copy(c, i).start()
            return carry

        lax.fori_loop(1, n_seq, send, 0)
        far_rows_in[c, 0:16, :] = far_rows[c, pl.ds(aligned(m * 16, 16), 16), :]

    def from_next(c):
        for t in range(tiles):
            query_copy(c, t).wait_recv()
        stat_copy(c).wait_recv()
        for kind in range(2):
            qc_t[kind] = qn[c, kind].T
        there = block < n_blocks - 1

        def step(i, carry):
            window = pl.ds(pair_window(i), WINDOW)
            pad_heads(i, 0)
            pad_heads(i, 1)
            js = [i * PAIR + u for u in range(PAIR)]
            level = jnp.concatenate([stat_next[c, pl.ds(j, 1), :] for j in js], axis=1)
            delta = jnp.concatenate([stat_next[c, pl.ds(heads + j, 1), :] for j in js], axis=1)
            s = dot(kv[c, 0, rows : 2 * rows, window], padded[0])
            s = jnp.where(there, s, FLOOR)
            p = jnp.exp2(s * to_log2 - level)
            dprob = dot(kv[c, 1, rows : 2 * rows, window], padded[1])
            ds = (p * (dprob - delta)).astype(BF16)
            own[c, 0, :, window] += dot(ds, stacked(qn[c, 0, :, window], i))
            own[c, 1, :, window] += dot(p.astype(BF16), stacked(qn[c, 1, :, window], i))
            return carry

        lax.fori_loop(0, heads // PAIR, step, 0)

    def finish(c):
        for d in range(1, y_n):
            mid_y_copy(c, d).wait_recv()

        def arrived(i, carry):
            far_row_copy(c, i).wait_recv()
            return carry

        lax.fori_loop(1, n_seq, arrived, 0)
        far_sum = far_rows_in[c, 0:16, :]
        for i in range(1, n_seq):
            far_sum = far_sum + far_rows_in[c, i * 16 : (i + 1) * 16, :]
        mine = pl.ds(aligned(yy * coarse, coarse), coarse)
        for kind in range(2):
            factor = scale if kind == 0 else 1.0
            added = mid_x[c, kind, mine, :].astype(F32)
            for d in range(1, y_n):
                added = added + mid_y_in[c, d - 1, kind].astype(F32)
            for t in range(tiles):
                cols = slice(t * TILE, (t + 1) * TILE)
                far = far_sum[kind * 8 + t : kind * 8 + t + 1, :] / math.sqrt(coarse)
                spread = (added[:, cols] + far) * (factor / math.sqrt(POOL))
                for i in range(coarse):
                    raw = own[c, kind, i * POOL : (i + 1) * POOL, cols] * factor
                    grad_rows[c, kind, i * POOL : (i + 1) * POOL, cols] = (
                        raw + spread[i : i + 1, :]
                    ).astype(BF16)
        store(c, 2, grad_rows.at[c, 0], dk_hbm).start()
        store(c, 3, grad_rows.at[c, 1], dv_hbm).start()

    prepare_own(0)
    mid_ready(0)
    prepare(0, mid_at, mid_rows)
    forward_far(0)
    start_far(1)
    start_raw(0, 3, tiles)
    far_ready(0)
    prepare(0, far_at, n_far)
    main(0)
    send_parts(0)
    start_raw(1, tiles - 1, tiles)
    prepare_own(1)
    mid_ready(1)
    prepare(1, mid_at, mid_rows)
    far_ready(1)
    prepare(1, far_at, n_far)
    main(1)
    send_parts(1)
    send_far(1, 0)
    send_mid(0)
    send_far(1, 1)
    from_next(0)
    cross_far(0)
    send_mid(1)
    from_next(1)
    send_rows(0)
    cross_far(1)
    finish(0)
    send_rows(1)
    finish(1)

    across_copy(side_y).wait_send()
    for copy in y_copies + x_copies:
        copy.wait_send()
    for c in range(HALVES):
        for t in range(tiles):
            key_copy(c, t).wait_send()
            query_copy(c, t).wait_send()
        pair_copy(c).wait_send()
        stat_copy(c).wait_send()
        cross_copy(c).wait_send()
        core_copy(c, 0).wait_send()
        core_copy(c, 1).wait_send()
        for d in range(1, x_n):
            mid_x_copy(c, d).wait_send()
        for d in range(1, y_n):
            mid_y_copy(c, d).wait_send()

        def left_z(i, carry, c=c):
            far_copy(c, i, zz, z_id(i)).wait_send()
            far_z_copy(c, 0, i).wait_send()
            far_z_copy(c, 1, i).wait_send()
            return carry

        def left_rows(i, carry, c=c):
            far_row_copy(c, i).wait_send()
            if c == 0:
                row_copy(i, m, (g, (m + i) % n_seq)).wait_send()
            return carry

        lax.fori_loop(1, z_n, left_z, 0)
        lax.fori_loop(1, n_seq, left_rows, 0)
        store(c, 0, out_rows.at[c, 0], o_hbm).wait()
        store(c, 1, out_rows.at[c, 1], dq_hbm).wait()
        store(c, 2, grad_rows.at[c, 0], dk_hbm).wait()
        store(c, 3, grad_rows.at[c, 1], dv_hbm).wait()


def hand_over(a, b, c, d, to_a, to_b, to_c, to_d):
    for src, dst in ((a, to_a), (b, to_b), (c, to_c), (d, to_d)):
        dst[...] = src[...]


def body(query, keys, values, cotangent):
    rows, width = query.shape
    n_seq = lax.axis_size("seq")
    n_grp = lax.axis_size("grp")
    part = width // HALVES
    coarse = rows // POOL
    mid_rows = n_seq * coarse
    n_far = n_grp * n_seq
    half = n_far // 2
    total = 2 * rows + mid_rows + n_far
    y_n = math.isqrt(n_seq)
    x_n = n_seq // y_n
    z_n = n_grp // 4
    heads = HEADS // HALVES
    tiles = part // TILE
    vmem = pltpu.VMEM
    dma = pltpu.SemaphoreType.DMA
    scratch = [
        vmem((HALVES, 2, total, part), BF16),
        vmem((HALVES, 2, rows, part), BF16),
        vmem((HALVES, 2, rows, part), BF16),
        vmem((2, part, total), BF16),
        vmem((2, part, rows), BF16),
        vmem((total, rows), F32),
        vmem((total, PAIR * rows), F32),
        vmem((total, PAIR * rows), BF16),
        vmem((total, PAIR * rows), BF16),
        vmem((part, rows), BF16),
        vmem((part, rows), BF16),
        vmem((HALVES, 2, rows, part), BF16),
        vmem((HALVES, 2 * heads, rows), F32),
        vmem((HALVES, 2 * heads, rows), F32),
        vmem((HALVES, 2, rows, part), F32),
        vmem((HALVES, 2, mid_rows, part), BF16),
        vmem((HALVES, 2, n_far, part), BF16),
        vmem((HALVES, 2, half, part), BF16),
        vmem((HALVES, 2, half, part), BF16),
        vmem((HALVES, z_n, 2, 2 * n_seq, part), BF16),
        vmem((HALVES, n_seq * 16, TILE), F32),
        vmem((HALVES, n_seq * 16, TILE), F32),
        vmem((HALVES, x_n - 1, 2, y_n * coarse, part), BF16),
        vmem((HALVES, 2, y_n * coarse, part), BF16),
        vmem((HALVES, y_n - 1, 2, coarse, part), BF16),
        vmem((HALVES, 2, rows, part), BF16),
        vmem((32, TILE), F32),
        vmem((n_seq * 32, TILE), F32),
        vmem((2, WINDOW, PAIR * rows), BF16),
        vmem((HALVES, 2, n_seq, part), F32),
        vmem((HALVES, 2, n_seq, part), F32),
        vmem((2, 2, n_seq, part), F32),
        vmem((HALVES, 2, n_seq, part), F32),
        dma((HALVES * 4,)),
        dma((1,)), dma((1,)),
        dma((HALVES,)), dma((HALVES,)),
        dma((n_seq,)), dma((n_seq,)),
        dma((y_n,)), dma((y_n,)),
        dma((HALVES, tiles)), dma((HALVES, tiles)),
        dma((HALVES, tiles)), dma((HALVES, tiles)),
        dma((HALVES, x_n)), dma((HALVES, x_n)),
        dma((HALVES, z_n)), dma((HALVES, z_n)),
        dma((HALVES,)), dma((HALVES,)),
        dma((HALVES,)), dma((HALVES,)),
        dma((HALVES, 2)), dma((HALVES, 2)),
        dma((HALVES, x_n)), dma((HALVES, x_n)),
        dma((HALVES, y_n)), dma((HALVES, y_n)),
        dma((HALVES, 2, z_n)), dma((HALVES, 2, z_n)),
        dma((HALVES, n_seq)), dma((HALVES, n_seq)),
        dma((HALVES * 4,)),
    ]
    flops = 12 * rows * total * width
    results = pl.pallas_call(
        functools.partial(kernel, n_grp, n_seq),
        out_shape=[jax.ShapeDtypeStruct((rows, width), BF16)] * 4,
        in_specs=[pl.BlockSpec(memory_space=pl.ANY)] * 4,
        out_specs=[pl.BlockSpec(memory_space=pl.ANY)] * 4,
        scratch_shapes=scratch,
        compiler_params=pltpu.CompilerParams(
            collective_id=0, has_side_effects=True, vmem_limit_bytes=60 * 2**20
        ),
        cost_estimate=pl.CostEstimate(
            flops=flops, bytes_accessed=16 * rows * width, transcendentals=HEADS * rows * total
        ),
    )(query, keys, values, cotangent)
    block = pl.BlockSpec((rows // 4, width), lambda i: (i, 0))
    return pl.pallas_call(
        hand_over,
        grid=(4,),
        out_shape=[jax.ShapeDtypeStruct((rows, width), BF16)] * 4,
        in_specs=[block] * 4,
        out_specs=[block] * 4,
        cost_estimate=pl.CostEstimate(flops=0, bytes_accessed=16 * rows * width, transcendentals=0),
        compiler_params=pltpu.CompilerParams(vmem_limit_bytes=60 * 2**20),
    )(*results)


def solution(mesh):
    spec = P(("grp", "seq"), None)
    return jax.shard_map(
        body, mesh=mesh, in_specs=(spec,) * 4, out_specs=(spec,) * 4, check_vma=False
    )
```
